32 devices in a mesh: dp: 16 (over z, x, core), tensor: 2 (over y).
Axes of the slice: x: 2, y: 2, z: 4, core: 2. Of those that a mesh axis runs over, the one named last changes fastest.
Arguments:
- tokens: bfloat16 [16, 256, 8192], P('dp', None, 'tensor'), may hold values from -6 to 6
- segment_ids: int32 [16, 256], P('dp'), may hold values from 0 to 3, never falling along the last dimension, each value on 1 to 128 neighbouring positions
- queries: bfloat16 [16, 256, 8192], P('dp', None, 'tensor'), may hold values from -7 to 7
- teacher_keys: bfloat16 [16, 256, 1024], P('dp', None, 'tensor'), may hold values from -7 to 7
- teacher_values: bfloat16 [16, 256, 1024], P('dp', None, 'tensor'), may hold values from -6 to 6
- down_weight: bfloat16 [8192, 512], P('tensor'), may hold values from -0.0625 to 0.0625
- rope_weight: bfloat16 [64, 8192], P(None, 'tensor'), may hold values from -1 to 1
- key_up: bfloat16 [512, 4096], P(None, 'tensor'), may hold values from -0.25 to 0.25
- value_up: bfloat16 [512, 8192], P(None, 'tensor'), may hold values from -0.25 to 0.25
Outputs:
- grad_down: float32 [8192, 512], P('tensor')
- grad_rope: float32 [64, 8192], P(None, 'tensor')
- grad_key_up: float32 [512, 4096], P(None, 'tensor')
- grad_value_up: float32 [512, 8192], P(None, 'tensor')
The draws below stay inside these ranges and needn't reach their ends.
Inputs may be any that keep to these rules, and one draw needn't show every extreme that they name: `segment_ids`: along a sequence the document number never falls; each of the 4 documents holds 1 to 128 tokens, and one holds exactly 128.
All inputs are finite; a program needn't handle non-finite values.
Results may differ from the reference program's by a relative error of at most 0.011.
Values sent between devices are 32-bit elements; how exact they have to be, the bound alone decides.
A program may use at most 128 MiB of HBM per device.

```python
import math
import jax
import jax.numpy as jnp
import numpy as np
from jax import lax

D = 8192
HEADS = 64
KVH = 8
HEAD = 128
LATENT = 512
ROPE = 64
SEQ = 256
DOCS = 4
SEQS = 16


plant_strengths = (4.0, 5.5, 7.0)


key_size = 7.0


token_size = 4.0


rope_pull = 3.0


def entry_masks():
    entry_index = jnp.arange(HEAD, dtype=jnp.int32)
    teacher_low = entry_index % (HEAD // 2) >= HEAD // 8
    rope_low = entry_index % (ROPE // 2) >= ROPE // 8
    in_rope = entry_index < ROPE
    planted = teacher_low & jnp.where(in_rope, rope_low, True)
    return (planted, planted & in_rope)


def sign_pattern(key):
    coin_flips = jax.random.randint(jax.random.fold_in(key, 101), (HEAD,), 0, 2)
    return (2 * coin_flips - 1).astype(jnp.float32)


def token_direction(key):
    coin_flips = jax.random.randint(jax.random.fold_in(key, 102), (D,), 0, 2)
    return (2 * coin_flips - 1).astype(jnp.float32)


def plant_positions(key):
    quarter = SEQ // 4
    offsets = jax.random.randint(jax.random.fold_in(key, 103), (SEQS, 3), 0, quarter - 3)
    return jnp.arange(3, dtype=jnp.int32)[None, :] * quarter + 2 + offsets


def row_hits(key, shift):
    plant_rows = plant_positions(key) - shift
    position = jnp.arange(SEQ, dtype=jnp.int32)
    return (position[None, :, None] == plant_rows[:, None, :]).astype(jnp.float32)


def clipped_normal(key, array_shape):
    return jnp.clip(jax.random.normal(key, array_shape, jnp.float32), -6.0, 6.0)


def draw_queries(key, part):
    planted, rope_planted = entry_masks()
    sign_row = sign_pattern(key)
    strengths = jnp.array(plant_strengths, jnp.float32)
    main_hits = row_hits(key, 0)
    row_strength = jnp.sum(main_hits * strengths[None, None, :], axis=-1)
    row_planted = jnp.sum(main_hits, axis=-1) > 0.5
    entry_scale = jnp.where(rope_planted, 1.0, jnp.where(planted, 2.0 / 3.0, 0.0)) * sign_row
    noise_part = clipped_normal(jax.random.fold_in(key, 1), (SEQS, SEQ, HEADS, HEAD))
    plant_value = jnp.where(planted[None, None, None, :], row_strength[:, :, None, None] * entry_scale[None, None, None, :], 0.1 * noise_part)
    values = jnp.where(row_planted[:, :, None, None], plant_value, noise_part)
    return values.reshape(SEQS, SEQ, HEADS * HEAD).astype(jnp.bfloat16)


def draw_teacher_keys(key, part):
    planted, unused_mask = entry_masks()
    sign_row = sign_pattern(key)
    main_planted = jnp.sum(row_hits(key, 0), axis=-1) > 0.5
    prev_planted = jnp.sum(row_hits(key, 1), axis=-1) > 0.5
    entry_index = jnp.arange(HEAD, dtype=jnp.int32)
    prev_entries = planted & (entry_index < HEAD - 1)
    noise_part = clipped_normal(jax.random.fold_in(key, 2), (SEQS, SEQ, KVH, HEAD))
    main_value = jnp.where(planted[None, None, None, :], key_size * sign_row[None, None, None, :], 0.1 * noise_part)
    prev_value = jnp.where(prev_entries[None, None, None, :], key_size * sign_row[None, None, None, :], 0.1 * noise_part)
    values = jnp.where(main_planted[:, :, None, None], main_value, jnp.where(prev_planted[:, :, None, None], prev_value, noise_part))
    return values.reshape(SEQS, SEQ, KVH * HEAD).astype(jnp.bfloat16)


def draw_tokens(key, part):
    unused_mask, rope_planted = entry_masks()
    rope_count = jnp.sum(rope_planted.astype(jnp.float32))
    strengths = jnp.array(plant_strengths, jnp.float32)
    row_gain = strengths * rope_pull * rope_count / math.sqrt(HEAD)
    prev_size = token_size - 2.0 / row_gain
    main_hits = row_hits(key, 0)
    prev_hits = row_hits(key, 1)
    row_scale = jnp.sum(main_hits * token_size + prev_hits * prev_size[None, None, :], axis=-1)
    row_planted = jnp.sum(main_hits + prev_hits, axis=-1) > 0.5
    direction = token_direction(key)
    noise_part = clipped_normal(jax.random.fold_in(key, 3), (SEQS, SEQ, D))
    values = jnp.where(row_planted[:, :, None], row_scale[:, :, None] * direction[None, None, :] + 0.15 * noise_part, noise_part)
    return values.astype(jnp.bfloat16)


def draw_rope_weight(key, part):
    unused_mask, rope_planted = entry_masks()
    sign_row = sign_pattern(key)
    pull_rows = jnp.where(rope_planted[:ROPE], rope_pull, 0.0) * sign_row[:ROPE]
    direction = token_direction(key)
    noise_part = clipped_normal(jax.random.fold_in(key, 4), (ROPE, D)) / math.sqrt(D)
    return (noise_part + pull_rows[:, None] * direction[None, :] / D).astype(jnp.bfloat16)


def shard_levels(own_key, shape, pieces, smallest, high):
    loudness, own = 1.0, jax.random.fold_in(own_key, 6)
    for dim, parts in pieces:
        heights = jnp.exp(jax.random.uniform(jax.random.fold_in(own, dim), (parts,), jnp.float32, smallest / len(pieces), high / len(pieces)))
        loudness = loudness * jnp.repeat(heights, shape[dim] // parts).reshape([-1 if axis == dim else 1 for axis in range(len(shape))])
    return loudness


def split_up(amount, total, most, slope):
    loads = [(1 << 20) // math.isqrt(rank ** slope) + 1 for rank in range(2, amount + 1)]
    spare, counts = total - most - (amount - 1), [1] * (amount - 1)
    while spare > 0:
        free = [i for i in range(amount - 1) if counts[i] < most]
        whole, remaining = sum([loads[i] for i in free]), spare
        for i in free:
            more = min(most - counts[i], max(1, remaining * loads[i] // whole), spare)
            counts[i] = counts[i] + more
            spare = spare - more
    return np.array([most] + counts)


def ragged(key, amount, total, bound, slope):
    if amount == 2:
        one = jax.random.randint(key, (), max(1, total - bound), min(bound, total - 1) + 1)
        return jnp.stack([one, total - one])
    sizes = jnp.asarray(split_up(amount, total, bound, slope), jnp.int32)
    couples = (amount - 1) // 2
    source_of, receiver = sizes[1:1 + 2 * couples:2], sizes[2:2 + 2 * couples:2]
    slack = jnp.minimum(source_of - 1, bound - receiver)
    passed = jax.random.randint(jax.random.fold_in(key, 1), (couples,), 0, 1 << 20) % (slack + 1)
    sizes = sizes.at[1:1 + 2 * couples:2].set(source_of - passed).at[2:2 + 2 * couples:2].set(receiver + passed)
    return sizes[jax.random.permutation(jax.random.fold_in(key, 2), amount)]


def gaussian(stream_key, dims, scale, limit, pieces=(), held_as=jnp.bfloat16):
    result = jax.random.normal(stream_key, dims, jnp.float32) * scale
    if len(pieces) > 0:
        result = shard_levels(stream_key, dims, pieces, -0.22, 0.18) * result
    return jnp.clip(result, min=-limit, max=limit).astype(held_as)


def setup_inputs(seed: int = 0) -> dict:
    splits = jax.random.split(jax.random.key(seed), 10)
    tokens = draw_tokens(jax.random.fold_in(splits[9], 71), 0)
    segment_ids = jax.vmap(lambda own: jnp.searchsorted(jnp.cumsum(ragged(own, DOCS, SEQ, SEQ // 2, 2)), jnp.arange(SEQ), side="right"))(jax.random.split(splits[1], SEQS)).reshape((SEQS, SEQ)).astype(jnp.int32)
    queries = draw_queries(jax.random.fold_in(splits[9], 71), 0)
    teacher_keys = draw_teacher_keys(jax.random.fold_in(splits[9], 71), 0)
    teacher_values = gaussian(splits[4], (SEQS, SEQ, KVH * HEAD), 1.0, 6.0, ((0, 16), (2, 2)))
    down_weight = gaussian(splits[5], (D, LATENT), D ** -0.5, 0.0625, ((0, 2),))
    rope_weight = draw_rope_weight(jax.random.fold_in(splits[9], 71), 0)
    key_up = gaussian(splits[7], (LATENT, HEADS * (HEAD - ROPE)), LATENT ** -0.5, 0.25, ((1, 2),))
    value_up = gaussian(splits[8], (LATENT, HEADS * HEAD), LATENT ** -0.5, 0.25, ((1, 2),))
    return dict(tokens=tokens, segment_ids=segment_ids, queries=queries, teacher_keys=teacher_keys, teacher_values=teacher_values, down_weight=down_weight, rope_weight=rope_weight, key_up=key_up, value_up=value_up)


theta_base = 500000.0
norm_eps = 1e-06

def angle_tables(positions, width):
    half_width = width // 2
    exponent = jnp.arange(half_width, dtype=jnp.float32) * (2.0 / width)
    frequency = jnp.exp(-exponent * jnp.log(jnp.float32(theta_base)))
    angles = positions.astype(jnp.float32)[:, None] * frequency[None, :]
    return (jnp.cos(angles), jnp.sin(angles))

def rotate_last(tensor, cosine, sine_tab):
    half_width = tensor.shape[-1] // 2
    first_half = tensor[..., :half_width]
    second_half = tensor[..., half_width:]
    return jnp.concatenate([first_half * cosine - second_half * sine_tab, second_half * cosine + first_half * sine_tab], axis=-1)

def rotate_rows(matrix, cosine, sine_tab):
    half_width = matrix.shape[0] // 2
    first_half = matrix[:half_width]
    second_half = matrix[half_width:]
    return jnp.concatenate([first_half * cosine - second_half * sine_tab, second_half * cosine + first_half * sine_tab], axis=0)

def unrotate_rows(matrix, cosine, sine_tab):
    half_width = matrix.shape[0] // 2
    first_half = matrix[:half_width]
    second_half = matrix[half_width:]
    return jnp.concatenate([first_half * cosine + second_half * sine_tab, second_half * cosine - first_half * sine_tab], axis=0)

def doc_positions(segments_row):
    position_index = jnp.arange(segments_row.shape[0], dtype=jnp.int32)
    is_start = jnp.concatenate([jnp.ones((1,), dtype=jnp.bool_), segments_row[1:] != segments_row[:-1]])
    doc_start = lax.cummax(jnp.where(is_start, position_index, 0).astype(jnp.int32), axis=0)
    return position_index - doc_start

def masked_softmax(scores, doc_mask):
    masked = jnp.where(doc_mask > 0, scores, -jnp.inf)
    peak = lax.optimization_barrier(jnp.max(masked, axis=-1, keepdims=True))
    weights = jnp.exp(masked - peak)
    return weights / lax.optimization_barrier(jnp.sum(weights, axis=-1, keepdims=True))

def sequence_grads(token_rows, segments_row, queries_row, tkeys_row, tvalues_row, down_weight, rope_weight, key_up, value_up):
    seq_len = token_rows.shape[0]
    nope_width = HEAD - ROPE
    group_size = HEADS // KVH
    score_scale = 1.0 / math.sqrt(HEAD)
    f32 = jnp.float32
    bf16 = jnp.bfloat16
    positions = doc_positions(segments_row)
    position_index = jnp.arange(seq_len, dtype=jnp.int32)
    doc_mask = ((segments_row[:, None] == segments_row[None, :]) & (position_index[None, :] <= position_index[:, None])).astype(jnp.int32)
    cos_full, sin_full = angle_tables(positions, HEAD)
    cos_rope, sin_rope = angle_tables(positions, ROPE)
    latent_raw = jnp.dot(token_rows, down_weight, preferred_element_type=f32)
    inv_rms = lax.rsqrt(lax.optimization_barrier(jnp.mean(latent_raw * latent_raw, axis=-1, keepdims=True)) + norm_eps)
    normed = latent_raw * inv_rms
    latent = normed.astype(bf16)
    rope_raw = lax.dot_general(rope_weight, token_rows, (((1,), (1,)), ((), ())), preferred_element_type=f32)
    rope_key = rotate_rows(rope_raw, cos_rope.T, sin_rope.T).astype(bf16)
    head_queries = queries_row.reshape(seq_len, HEADS, HEAD).transpose(1, 0, 2)
    teacher_q = rotate_last(head_queries.astype(f32), cos_full, sin_full).astype(bf16).reshape(KVH, group_size, seq_len, HEAD)
    teacher_k = rotate_last(tkeys_row.reshape(seq_len, KVH, HEAD).transpose(1, 0, 2).astype(f32), cos_full, sin_full).astype(bf16)
    teacher_v = tvalues_row.reshape(seq_len, KVH, HEAD).transpose(1, 0, 2)
    teacher_scores = jnp.einsum('kgqd,kpd->kgqp', teacher_q.astype(f32), teacher_k.astype(f32)) * score_scale
    teacher_weights = masked_softmax(teacher_scores, doc_mask).astype(bf16)
    teacher_out = jnp.einsum('kgqp,kpd->kgqd', teacher_weights.astype(f32), teacher_v.astype(f32)).reshape(HEADS, seq_len, HEAD)
    key_nope = jnp.dot(latent, key_up, preferred_element_type=f32).astype(bf16).reshape(seq_len, HEADS, nope_width).transpose(1, 0, 2)
    head_values = jnp.dot(latent, value_up, preferred_element_type=f32).astype(bf16).reshape(seq_len, HEADS, HEAD).transpose(1, 0, 2)
    rotated_q = rotate_last(head_queries[..., :ROPE].astype(f32), cos_rope, sin_rope).astype(bf16)
    student_q = jnp.concatenate([head_queries[..., ROPE:], rotated_q], axis=-1)
    student_k = jnp.concatenate([key_nope, jnp.broadcast_to(rope_key.T[None], (HEADS, seq_len, ROPE))], axis=-1)
    student_scores = jnp.einsum('hqd,hpd->hqp', student_q.astype(f32), student_k.astype(f32)) * score_scale
    student_weights = masked_softmax(student_scores, doc_mask)
    student_low = student_weights.astype(bf16)
    student_out = jnp.einsum('hqp,hpd->hqd', student_low.astype(f32), head_values.astype(f32))
    out_grad = (student_out - teacher_out).astype(bf16)
    weight_grad = jnp.einsum('hqd,hpd->hqp', out_grad.astype(f32), head_values.astype(f32))
    row_dot = lax.optimization_barrier(jnp.sum(student_weights * weight_grad, axis=-1, keepdims=True))
    score_grad = (student_weights * (weight_grad - row_dot) * score_scale).astype(bf16)
    value_grad = jnp.einsum('hqp,hqd->hpd', student_low.astype(f32), out_grad.astype(f32)).astype(bf16)
    key_grad = jnp.einsum('hqp,hqd->hpd', score_grad.astype(f32), student_q.astype(f32))
    nope_grad = key_grad[..., :nope_width].astype(bf16).transpose(1, 0, 2).reshape(seq_len, HEADS * nope_width)
    rope_sum = lax.optimization_barrier(jnp.sum(key_grad[..., nope_width:], axis=0)).T
    rope_grad = unrotate_rows(rope_sum, cos_rope.T, sin_rope.T).astype(bf16)
    value_flat = value_grad.transpose(1, 0, 2).reshape(seq_len, HEADS * HEAD)
    contract_cols = (((1,), (1,)), ((), ()))
    contract_rows = (((0,), (0,)), ((), ()))
    norm_grad = lax.dot_general(nope_grad, key_up, contract_cols, preferred_element_type=f32) + lax.dot_general(value_flat, value_up, contract_cols, preferred_element_type=f32)
    latent_grad = ((norm_grad - normed * lax.optimization_barrier(jnp.mean(norm_grad * normed, axis=-1, keepdims=True))) * inv_rms).astype(bf16)
    grad_down = lax.dot_general(token_rows, latent_grad, contract_rows, preferred_element_type=f32)
    grad_rope = jnp.dot(rope_grad, token_rows, preferred_element_type=f32)
    grad_kup = lax.dot_general(latent, nope_grad, contract_rows, preferred_element_type=f32)
    grad_vup = lax.dot_general(latent, value_flat, contract_rows, preferred_element_type=f32)
    return (grad_down, grad_rope, grad_kup, grad_vup)

def reference(tokens, segment_ids, queries, teacher_keys, teacher_values, down_weight, rope_weight, key_up, value_up):

    def accumulate(running, row_inputs):
        token_rows, segments_row, queries_row, tkeys_row, tvalues_row = row_inputs
        new_grads = sequence_grads(token_rows, segments_row, queries_row, tkeys_row, tvalues_row, down_weight, rope_weight, key_up, value_up)
        return (tuple((old_sum + new_grad for old_sum, new_grad in zip(running, new_grads))), None)
    zeros_init = (jnp.zeros(down_weight.shape, jnp.float32), jnp.zeros(rope_weight.shape, jnp.float32), jnp.zeros(key_up.shape, jnp.float32), jnp.zeros(value_up.shape, jnp.float32))
    totals, unused = lax.scan(accumulate, zeros_init, (tokens, segment_ids, queries, teacher_keys, teacher_values))
    return (totals[0], totals[1], totals[2], totals[3])
```

```python
import math

import jax
import jax.numpy as jnp
from jax import lax
from jax.sharding import PartitionSpec as P

HEAD = 128
ROPE = 64


theta_base = 500000.0
norm_eps = 1e-06


def angle_tables(positions, width):
    half_width = width // 2
    exponent = jnp.arange(half_width, dtype=jnp.float32) * (2.0 / width)
    frequency = jnp.exp(-exponent * jnp.log(jnp.float32(theta_base)))
    angles = positions.astype(jnp.float32)[:, None] * frequency[None, :]
    return (jnp.cos(angles), jnp.sin(angles))


def rotate_last(tensor, cosine, sine_tab):
    half_width = tensor.shape[-1] // 2
    first_half = tensor[..., :half_width]
    second_half = tensor[..., half_width:]
    return jnp.concatenate(
        [
            first_half * cosine - second_half * sine_tab,
            second_half * cosine + first_half * sine_tab,
        ],
        axis=-1,
    )


def rotate_rows(matrix, cosine, sine_tab):
    half_width = matrix.shape[0] // 2
    first_half = matrix[:half_width]
    second_half = matrix[half_width:]
    return jnp.concatenate(
        [
            first_half * cosine - second_half * sine_tab,
            second_half * cosine + first_half * sine_tab,
        ],
        axis=0,
    )


def unrotate_rows(matrix, cosine, sine_tab):
    half_width = matrix.shape[0] // 2
    first_half = matrix[:half_width]
    second_half = matrix[half_width:]
    return jnp.concatenate(
        [
            first_half * cosine + second_half * sine_tab,
            second_half * cosine - first_half * sine_tab,
        ],
        axis=0,
    )


def doc_positions(segments_row):
    position_index = jnp.arange(segments_row.shape[0], dtype=jnp.int32)
    earlier = (segments_row[None, :] < segments_row[:, None]).astype(jnp.int32)
    return position_index - jnp.sum(earlier, axis=1)


def block_mask(seg_block, segments_row, row_start):
    rows_index = row_start + jnp.arange(seg_block.shape[0], dtype=jnp.int32)
    cols_index = jnp.arange(segments_row.shape[0], dtype=jnp.int32)
    return (
        (seg_block[:, None] == segments_row[None, :]) & (cols_index[None, :] <= rows_index[:, None])
    ).astype(jnp.int32)


def masked_softmax(scores, doc_mask):
    masked = jnp.where(doc_mask > 0, scores, -jnp.inf)
    peak = jnp.max(masked, axis=-1, keepdims=True)
    weights = jnp.exp(masked - peak)
    return weights / jnp.sum(weights, axis=-1, keepdims=True)


def local(
    tokens,
    segment_ids,
    queries,
    teacher_keys,
    teacher_values,
    down_weight,
    rope_weight,
    key_up,
    value_up,
):
    f32 = jnp.float32
    bf16 = jnp.bfloat16
    token_rows = tokens[0]
    segments_row = segment_ids[0]
    seq_len = token_rows.shape[0]
    heads_local = queries.shape[2] // HEAD
    kv_local = teacher_keys.shape[2] // HEAD
    group_size = heads_local // kv_local
    nope_width = HEAD - ROPE
    score_scale = 1.0 / math.sqrt(HEAD)
    contract_cols = (((1,), (1,)), ((), ()))
    contract_rows = (((0,), (0,)), ((), ()))
    positions = doc_positions(segments_row)
    cos_full, sin_full = angle_tables(positions, HEAD)
    cos_rope, sin_rope = angle_tables(positions, ROPE)
    latent_part = jnp.dot(token_rows, down_weight, preferred_element_type=f32)
    rope_part = lax.dot_general(rope_weight, token_rows, contract_cols, preferred_element_type=f32)
    latent_raw, rope_sum = lax.psum((latent_part, rope_part), "tensor")
    inv_rms = lax.rsqrt(jnp.mean(latent_raw * latent_raw, axis=-1, keepdims=True) + norm_eps)
    normed = latent_raw * inv_rms
    latent = normed.astype(bf16)
    rope_key = rotate_rows(rope_sum, cos_rope.T, sin_rope.T).astype(bf16)
    head_queries = queries[0].reshape(seq_len, heads_local, HEAD).transpose(1, 0, 2)
    teacher_q = (
        rotate_last(head_queries.astype(f32), cos_full, sin_full)
        .astype(bf16)
        .reshape(kv_local, group_size, seq_len, HEAD)
    )
    teacher_k = rotate_last(
        teacher_keys[0].reshape(seq_len, kv_local, HEAD).transpose(1, 0, 2).astype(f32),
        cos_full,
        sin_full,
    ).astype(bf16)
    teacher_v = teacher_values[0].reshape(seq_len, kv_local, HEAD).transpose(1, 0, 2)
    key_nope = (
        jnp.dot(latent, key_up, preferred_element_type=f32)
        .astype(bf16)
        .reshape(seq_len, heads_local, nope_width)
        .transpose(1, 0, 2)
    )
    head_values = (
        jnp.dot(latent, value_up, preferred_element_type=f32)
        .astype(bf16)
        .reshape(seq_len, heads_local, HEAD)
        .transpose(1, 0, 2)
    )
    rotated_q = rotate_last(head_queries[..., :ROPE].astype(f32), cos_rope, sin_rope).astype(bf16)
    student_q = jnp.concatenate([head_queries[..., ROPE:], rotated_q], axis=-1)
    student_k = jnp.concatenate(
        [key_nope, jnp.broadcast_to(rope_key.T[None], (heads_local, seq_len, ROPE))], axis=-1
    )
    block_rows = min(seq_len, 512)
    block_count = seq_len // block_rows

    def attend_block(carry, block_index):
        value_acc, key_acc = carry
        row_start = block_index * block_rows
        doc_mask = block_mask(segments_row, segments_row, row_start)
        teacher_scores = (
            jnp.einsum("kgqd,kpd->kgqp", teacher_q, teacher_k, preferred_element_type=f32)
            * score_scale
        )
        teacher_weights = masked_softmax(teacher_scores, doc_mask).astype(bf16)
        teacher_out = jnp.einsum(
            "kgqp,kpd->kgqd", teacher_weights, teacher_v, preferred_element_type=f32
        ).reshape(heads_local, block_rows, HEAD)
        student_scores = (
            jnp.einsum("hqd,hpd->hqp", student_q, student_k, preferred_element_type=f32)
            * score_scale
        )
        student_weights = masked_softmax(student_scores, doc_mask)
        student_low = student_weights.astype(bf16)
        student_out = jnp.einsum(
            "hqp,hpd->hqd", student_low, head_values, preferred_element_type=f32
        )
        out_grad = (student_out - teacher_out).astype(bf16)
        weight_grad = jnp.einsum("hqd,hpd->hqp", out_grad, head_values, preferred_element_type=f32)
        row_dot = jnp.sum(student_weights * weight_grad, axis=-1, keepdims=True)
        score_grad = (student_weights * (weight_grad - row_dot) * score_scale).astype(bf16)
        value_acc = value_acc + jnp.einsum(
            "hqp,hqd->hpd", student_low, out_grad, preferred_element_type=f32
        )
        key_acc = key_acc + jnp.einsum(
            "hqp,hqd->hpd", score_grad, student_q, preferred_element_type=f32
        )
        return ((value_acc, key_acc), None)

    zeros_acc = jnp.zeros((heads_local, seq_len, HEAD), f32)
    accums, unused = lax.scan(
        attend_block, (zeros_acc, zeros_acc), jnp.arange(block_count, dtype=jnp.int32)
    )
    value_acc, key_acc = accums
    value_flat = value_acc.astype(bf16).transpose(1, 0, 2).reshape(seq_len, heads_local * HEAD)
    nope_grad = (
        key_acc[..., :nope_width]
        .astype(bf16)
        .transpose(1, 0, 2)
        .reshape(seq_len, heads_local * nope_width)
    )
    rope_grad_part = jnp.sum(key_acc[..., nope_width:], axis=0).T
    norm_grad_part = lax.dot_general(
        nope_grad, key_up, contract_cols, preferred_element_type=f32
    ) + lax.dot_general(value_flat, value_up, contract_cols, preferred_element_type=f32)
    grad_kup = lax.dot_general(latent, nope_grad, contract_rows, preferred_element_type=f32)
    grad_vup = lax.dot_general(latent, value_flat, contract_rows, preferred_element_type=f32)
    norm_grad, rope_grad_sum = lax.psum((norm_grad_part, rope_grad_part), "tensor")
    latent_grad = (
        (norm_grad - normed * jnp.mean(norm_grad * normed, axis=-1, keepdims=True)) * inv_rms
    ).astype(bf16)
    rope_grad = unrotate_rows(rope_grad_sum, cos_rope.T, sin_rope.T).astype(bf16)
    grad_down = lax.dot_general(token_rows, latent_grad, contract_rows, preferred_element_type=f32)
    grad_rope = jnp.dot(rope_grad, token_rows, preferred_element_type=f32)
    grad_down, grad_rope, grad_kup, grad_vup = lax.psum(
        (grad_down, grad_rope, grad_kup, grad_vup), "dp"
    )
    return (grad_down, grad_rope, grad_kup, grad_vup)


def solution(mesh):
    in_specs = (
        P("dp", None, "tensor"),
        P("dp", None),
        P("dp", None, "tensor"),
        P("dp", None, "tensor"),
        P("dp", None, "tensor"),
        P("tensor", None),
        P(None, "tensor"),
        P(None, "tensor"),
        P(None, "tensor"),
    )
    out_specs = (P("tensor", None), P(None, "tensor"), P(None, "tensor"), P(None, "tensor"))
    return jax.shard_map(local, mesh=mesh, in_specs=in_specs, out_specs=out_specs, check_vma=False)
```

```python
import functools
import math

import jax
import jax.numpy as jnp
from jax import lax
from jax.experimental import pallas as pl
from jax.experimental.pallas import tpu as pltpu
from jax.sharding import PartitionSpec as P

HEAD = 128
ROPE = 64


theta_base = 500000.0
norm_eps = 1e-06


def angle_tables(positions, width):
    half_width = width // 2
    exponent = jnp.arange(half_width, dtype=jnp.float32) * (2.0 / width)
    frequency = jnp.exp(-exponent * jnp.log(jnp.float32(theta_base)))
    angles = positions.astype(jnp.float32)[:, None] * frequency[None, :]
    return (jnp.cos(angles), jnp.sin(angles))


def rotate_last(tensor, cosine, sine_tab):
    half_width = tensor.shape[-1] // 2
    first_half = tensor[..., :half_width]
    second_half = tensor[..., half_width:]
    return jnp.concatenate(
        [
            first_half * cosine - second_half * sine_tab,
            second_half * cosine + first_half * sine_tab,
        ],
        axis=-1,
    )


def rotate_rows(matrix, cosine, sine_tab):
    half_width = matrix.shape[0] // 2
    first_half = matrix[:half_width]
    second_half = matrix[half_width:]
    return jnp.concatenate(
        [
            first_half * cosine - second_half * sine_tab,
            second_half * cosine + first_half * sine_tab,
        ],
        axis=0,
    )


def unrotate_rows(matrix, cosine, sine_tab):
    half_width = matrix.shape[0] // 2
    first_half = matrix[:half_width]
    second_half = matrix[half_width:]
    return jnp.concatenate(
        [
            first_half * cosine + second_half * sine_tab,
            second_half * cosine - first_half * sine_tab,
        ],
        axis=0,
    )


def doc_positions(segments_row):
    position_index = jnp.arange(segments_row.shape[0], dtype=jnp.int32)
    earlier = (segments_row[None, :] < segments_row[:, None]).astype(jnp.int32)
    return position_index - jnp.sum(earlier, axis=1)


def block_mask(seg_block, segments_row, row_start):
    rows_index = row_start + jnp.arange(seg_block.shape[0], dtype=jnp.int32)
    cols_index = jnp.arange(segments_row.shape[0], dtype=jnp.int32)
    return (
        (seg_block[:, None] == segments_row[None, :]) & (cols_index[None, :] <= rows_index[:, None])
    ).astype(jnp.int32)


def masked_softmax(scores, doc_mask):
    masked = jnp.where(doc_mask > 0, scores, -jnp.inf)
    peak = jnp.max(masked, axis=-1, keepdims=True)
    weights = jnp.exp(masked - peak)
    return weights / jnp.sum(weights, axis=-1, keepdims=True)


CHUNKS = 21


def sum_kernel(chunks, g_ref, out_ref, acc, from_core, from_x, result, from_mid, *sems):
    (load_s, core_s, core_r, x_s, x_r, z_s, z_r, mid_s, mid_r) = sems[:9]
    (xg_s, xg_r, own_s, own_r, fwd_s, fwd_r, keep_s) = sems[9:]
    rows = acc.shape[1] // chunks
    me = lax.axis_index("dp")
    core = lax.rem(me, 2)
    x = lax.rem(me // 2, 2)
    z = me // 4
    other_core = me + 1 - 2 * core
    other_x = me + 2 - 4 * x
    pair_z = me + 4 - 8 * lax.rem(z, 2)
    other_mid = (3 - z) * 4 + lax.rem(me, 4)
    is_mid = (z == 1) | (z == 2)
    is_end = (z == 0) | (z == 3)

    def part(k):
        return pl.ds(pl.multiple_of(k * rows, rows), rows)

    def send(src, dst, s, r, k, to):
        return pltpu.make_async_remote_copy(
            src_ref=src,
            dst_ref=dst,
            send_sem=s.at[k],
            recv_sem=r.at[k],
            device_id={"dp": to},
            device_id_type=pl.DeviceIdType.MESH,
        )

    def load(k):
        return pltpu.make_async_copy(g_ref.at[:, core, part(k)], acc.at[:, part(k)], load_s.at[k])

    def core_copy(k):
        return send(
            g_ref.at[:, 1 - core, part(k)], from_core.at[:, part(k)], core_s, core_r, k, other_core
        )

    def x_copy(k):
        return send(acc.at[1 - x, part(k)], from_x.at[part(k)], x_s, x_r, k, other_x)

    def up_copy(k):
        return send(acc.at[x, part(k)], result.at[part(k)], z_s, z_r, k, pair_z)

    def mid_copy(k):
        return send(acc.at[x, part(k)], from_mid.at[part(k)], mid_s, mid_r, k, other_mid)

    def down_copy(k):
        return send(result.at[part(k)], result.at[part(k)], z_s, z_r, k, pair_z)

    def xg_copy(k):
        return send(result.at[part(k)], out_ref.at[x, core, part(k)], xg_s, xg_r, k, other_x)

    def own_copy(k):
        return send(result.at[part(k)], out_ref.at[x, core, part(k)], own_s, own_r, k, other_core)

    def keep(k):
        return pltpu.make_async_copy(
            result.at[part(k)], out_ref.at[x, core, part(k)], keep_s.at[k]
        )

    def fwd_copy(k):
        block = out_ref.at[1 - x, core, part(k)]
        return send(block, block, fwd_s, fwd_r, k, other_core)

    barrier = pltpu.get_barrier_semaphore()
    for device in (other_core, other_x, pair_z):
        pl.semaphore_signal(
            barrier, inc=1, device_id={"dp": device}, device_id_type=pl.DeviceIdType.MESH
        )

    @pl.when(is_mid)
    def _():
        pl.semaphore_signal(
            barrier, inc=1, device_id={"dp": other_mid}, device_id_type=pl.DeviceIdType.MESH
        )
        pl.semaphore_wait(barrier, 4)

    @pl.when(is_end)
    def _():
        pl.semaphore_wait(barrier, 3)

    def stage0(k):
        load(k).start()
        core_copy(k).start()

    def stage1(k):
        load(k).wait()
        core_copy(k).wait_recv()
        acc[:, part(k), :] = acc[:, part(k), :] + from_core[:, part(k), :]
        x_copy(k).start()

    def stage2(k):
        x_copy(k).wait_recv()
        acc[x, part(k), :] = acc[x, part(k), :] + from_x[part(k), :]

        @pl.when(is_end)
        def _():
            up_copy(k).start()

    def stage3(k):
        @pl.when(is_mid)
        def _():
            up_copy(k).wait_recv()
            acc[x, part(k), :] = acc[x, part(k), :] + result[part(k), :]
            mid_copy(k).start()

    def stage4(k):
        @pl.when(is_mid)
        def _():
            mid_copy(k).wait_recv()
            result[part(k), :] = acc[x, part(k), :] + from_mid[part(k), :]
            down_copy(k).start()

    def stage5(k):
        @pl.when(is_end)
        def _():
            down_copy(k).wait_recv()

        xg_copy(k).start()
        own_copy(k).start()
        keep(k).start()

    def stage6(k):
        send(
            result.at[part(k)], out_ref.at[1 - x, core, part(k)], xg_s, xg_r, k, other_x
        ).wait_recv()
        fwd_copy(k).start()

    stages = (stage0, stage1, stage2, stage3, stage4, stage5, stage6)

    @pl.loop(0, chunks + len(stages) - 1)
    def _(t):
        for lag in reversed(range(len(stages))):
            @pl.when((t >= lag) & (t < chunks + lag))
            def _():
                stages[lag](t - lag)

    @pl.loop(0, chunks)
    def _(k):
        core_copy(k).wait_send()
        x_copy(k).wait_send()

        @pl.when(is_end)
        def _():
            up_copy(k).wait_send()

        @pl.when(is_mid)
        def _():
            mid_copy(k).wait_send()
            down_copy(k).wait_send()

        xg_copy(k).wait_send()
        own_copy(k).wait_send()
        keep(k).wait()
        fwd_copy(k).wait_send()
        send(
            result.at[part(k)], out_ref.at[x, 1 - core, part(k)], own_s, own_r, k, other_core
        ).wait_recv()
        send(
            result.at[part(k)], out_ref.at[1 - x, 1 - core, part(k)], fwd_s, fwd_r, k, other_core
        ).wait_recv()


def sum_rows(rows):
    count, width = rows.shape
    quarter = count // 4
    f32 = jnp.float32
    dma = pltpu.SemaphoreType.DMA((CHUNKS,))
    out = pl.pallas_call(
        functools.partial(sum_kernel, CHUNKS),
        out_shape=jax.ShapeDtypeStruct((2, 2, quarter, width), f32),
        in_specs=[pl.BlockSpec(memory_space=pl.ANY)],
        out_specs=pl.BlockSpec(memory_space=pl.ANY),
        scratch_shapes=[
            pltpu.VMEM((2, quarter, width), f32),
            pltpu.VMEM((2, quarter, width), f32),
            pltpu.VMEM((quarter, width), f32),
            pltpu.VMEM((quarter, width), f32),
            pltpu.VMEM((quarter, width), f32),
        ]
        + [dma] * 16,
        compiler_params=pltpu.CompilerParams(
            collective_id=0, has_side_effects=True, vmem_limit_bytes=56 * 2**20
        ),
    )(rows.reshape(2, 2, quarter, width))
    return out.reshape(count, width)


def sum_grads(grads):
    width = 512
    blocks, counts = [], []
    for grad in grads:
        pieces = [grad[:, i : i + width] for i in range(0, grad.shape[1], width)]
        counts.append(len(pieces))
        blocks += pieces
    total = sum_rows(jnp.concatenate(blocks, axis=0))
    outs, start = [], 0
    for grad, count in zip(grads, counts):
        pieces = []
        for _ in range(count):
            pieces.append(total[start : start + grad.shape[0]])
            start += grad.shape[0]
        outs.append(jnp.concatenate(pieces, axis=1))
    return tuple(outs)


def local(
    by_kernel,
    tokens,
    segment_ids,
    queries,
    teacher_keys,
    teacher_values,
    down_weight,
    rope_weight,
    key_up,
    value_up,
):
    f32 = jnp.float32
    bf16 = jnp.bfloat16
    token_rows = tokens[0]
    segments_row = segment_ids[0]
    seq_len = token_rows.shape[0]
    heads_local = queries.shape[2] // HEAD
    kv_local = teacher_keys.shape[2] // HEAD
    group_size = heads_local // kv_local
    nope_width = HEAD - ROPE
    score_scale = 1.0 / math.sqrt(HEAD)
    contract_cols = (((1,), (1,)), ((), ()))
    contract_rows = (((0,), (0,)), ((), ()))
    positions = doc_positions(segments_row)
    cos_full, sin_full = angle_tables(positions, HEAD)
    cos_rope, sin_rope = angle_tables(positions, ROPE)
    latent_part = jnp.dot(token_rows, down_weight, preferred_element_type=f32)
    rope_part = lax.dot_general(rope_weight, token_rows, contract_cols, preferred_element_type=f32)
    latent_raw, rope_sum = lax.psum((latent_part, rope_part), "tensor")
    inv_rms = lax.rsqrt(jnp.mean(latent_raw * latent_raw, axis=-1, keepdims=True) + norm_eps)
    normed = latent_raw * inv_rms
    latent = normed.astype(bf16)
    rope_key = rotate_rows(rope_sum, cos_rope.T, sin_rope.T).astype(bf16)
    head_queries = queries[0].reshape(seq_len, heads_local, HEAD).transpose(1, 0, 2)
    teacher_q = (
        rotate_last(head_queries.astype(f32), cos_full, sin_full)
        .astype(bf16)
        .reshape(kv_local, group_size, seq_len, HEAD)
    )
    teacher_k = rotate_last(
        teacher_keys[0].reshape(seq_len, kv_local, HEAD).transpose(1, 0, 2).astype(f32),
        cos_full,
        sin_full,
    ).astype(bf16)
    teacher_v = teacher_values[0].reshape(seq_len, kv_local, HEAD).transpose(1, 0, 2)
    key_nope = (
        jnp.dot(latent, key_up, preferred_element_type=f32)
        .astype(bf16)
        .reshape(seq_len, heads_local, nope_width)
        .transpose(1, 0, 2)
    )
    head_values = (
        jnp.dot(latent, value_up, preferred_element_type=f32)
        .astype(bf16)
        .reshape(seq_len, heads_local, HEAD)
        .transpose(1, 0, 2)
    )
    rotated_q = rotate_last(head_queries[..., :ROPE].astype(f32), cos_rope, sin_rope).astype(bf16)
    student_q = jnp.concatenate([head_queries[..., ROPE:], rotated_q], axis=-1)
    student_k = jnp.concatenate(
        [key_nope, jnp.broadcast_to(rope_key.T[None], (heads_local, seq_len, ROPE))], axis=-1
    )
    block_rows = min(seq_len, 512)
    block_count = seq_len // block_rows

    def attend_block(carry, block_index):
        value_acc, key_acc = carry
        row_start = block_index * block_rows
        doc_mask = block_mask(segments_row, segments_row, row_start)
        teacher_scores = (
            jnp.einsum("kgqd,kpd->kgqp", teacher_q, teacher_k, preferred_element_type=f32)
            * score_scale
        )
        teacher_weights = masked_softmax(teacher_scores, doc_mask).astype(bf16)
        teacher_out = jnp.einsum(
            "kgqp,kpd->kgqd", teacher_weights, teacher_v, preferred_element_type=f32
        ).reshape(heads_local, block_rows, HEAD)
        student_scores = (
            jnp.einsum("hqd,hpd->hqp", student_q, student_k, preferred_element_type=f32)
            * score_scale
        )
        student_weights = masked_softmax(student_scores, doc_mask)
        student_low = student_weights.astype(bf16)
        student_out = jnp.einsum(
            "hqp,hpd->hqd", student_low, head_values, preferred_element_type=f32
        )
        out_grad = (student_out - teacher_out).astype(bf16)
        weight_grad = jnp.einsum("hqd,hpd->hqp", out_grad, head_values, preferred_element_type=f32)
        row_dot = jnp.sum(student_weights * weight_grad, axis=-1, keepdims=True)
        score_grad = (student_weights * (weight_grad - row_dot) * score_scale).astype(bf16)
        value_acc = value_acc + jnp.einsum(
            "hqp,hqd->hpd", student_low, out_grad, preferred_element_type=f32
        )
        key_acc = key_acc + jnp.einsum(
            "hqp,hqd->hpd", score_grad, student_q, preferred_element_type=f32
        )
        return ((value_acc, key_acc), None)

    zeros_acc = jnp.zeros((heads_local, seq_len, HEAD), f32)
    accums, unused = lax.scan(
        attend_block, (zeros_acc, zeros_acc), jnp.arange(block_count, dtype=jnp.int32)
    )
    value_acc, key_acc = accums
    value_flat = value_acc.astype(bf16).transpose(1, 0, 2).reshape(seq_len, heads_local * HEAD)
    nope_grad = (
        key_acc[..., :nope_width]
        .astype(bf16)
        .transpose(1, 0, 2)
        .reshape(seq_len, heads_local * nope_width)
    )
    rope_grad_part = jnp.sum(key_acc[..., nope_width:], axis=0).T
    norm_grad_part = lax.dot_general(
        nope_grad, key_up, contract_cols, preferred_element_type=f32
    ) + lax.dot_general(value_flat, value_up, contract_cols, preferred_element_type=f32)
    grad_kup = lax.dot_general(latent, nope_grad, contract_rows, preferred_element_type=f32)
    grad_vup = lax.dot_general(latent, value_flat, contract_rows, preferred_element_type=f32)
    norm_grad, rope_grad_sum = lax.psum((norm_grad_part, rope_grad_part), "tensor")
    latent_grad = (
        (norm_grad - normed * jnp.mean(norm_grad * normed, axis=-1, keepdims=True)) * inv_rms
    ).astype(bf16)
    rope_grad = unrotate_rows(rope_grad_sum, cos_rope.T, sin_rope.T).astype(bf16)
    grad_down = lax.dot_general(token_rows, latent_grad, contract_rows, preferred_element_type=f32)
    grad_rope = jnp.dot(rope_grad, token_rows, preferred_element_type=f32)
    grads = (grad_down, grad_rope, grad_kup, grad_vup)
    if by_kernel:
        return sum_grads(grads)
    return lax.psum(grads, "dp")


def solution(mesh):
    in_specs = (
        P("dp", None, "tensor"),
        P("dp", None),
        P("dp", None, "tensor"),
        P("dp", None, "tensor"),
        P("dp", None, "tensor"),
        P("tensor", None),
        P(None, "tensor"),
        P(None, "tensor"),
        P(None, "tensor"),
    )
    out_specs = (P("tensor", None), P(None, "tensor"), P(None, "tensor"), P(None, "tensor"))
    by_kernel = mesh.shape["dp"] == 16 and mesh.shape["tensor"] == 2
    body = functools.partial(local, by_kernel)
    return jax.shard_map(body, mesh=mesh, in_specs=in_specs, out_specs=out_specs, check_vma=False)
```

```python
import functools
import math

import jax
import jax.numpy as jnp
from jax import lax
from jax.experimental import pallas as pl
from jax.experimental.pallas import tpu as pltpu
from jax.sharding import PartitionSpec as P

HEAD = 128
ROPE = 64


theta_base = 500000.0
norm_eps = 1e-06


def angle_tables(positions, width):
    half_width = width // 2
    exponent = jnp.arange(half_width, dtype=jnp.float32) * (2.0 / width)
    frequency = jnp.exp(-exponent * jnp.log(jnp.float32(theta_base)))
    angles = positions.astype(jnp.float32)[:, None] * frequency[None, :]
    return (jnp.cos(angles), jnp.sin(angles))


def rotate_last(tensor, cosine, sine_tab):
    half_width = tensor.shape[-1] // 2
    first_half = tensor[..., :half_width]
    second_half = tensor[..., half_width:]
    return jnp.concatenate(
        [
            first_half * cosine - second_half * sine_tab,
            second_half * cosine + first_half * sine_tab,
        ],
        axis=-1,
    )


def rotate_rows(matrix, cosine, sine_tab):
    half_width = matrix.shape[0] // 2
    first_half = matrix[:half_width]
    second_half = matrix[half_width:]
    return jnp.concatenate(
        [
            first_half * cosine - second_half * sine_tab,
            second_half * cosine + first_half * sine_tab,
        ],
        axis=0,
    )


def unrotate_rows(matrix, cosine, sine_tab):
    half_width = matrix.shape[0] // 2
    first_half = matrix[:half_width]
    second_half = matrix[half_width:]
    return jnp.concatenate(
        [
            first_half * cosine + second_half * sine_tab,
            second_half * cosine - first_half * sine_tab,
        ],
        axis=0,
    )


def doc_positions(segments_row):
    position_index = jnp.arange(segments_row.shape[0], dtype=jnp.int32)
    earlier = (segments_row[None, :] < segments_row[:, None]).astype(jnp.int32)
    return position_index - jnp.sum(earlier, axis=1)


def block_mask(seg_block, segments_row, row_start):
    rows_index = row_start + jnp.arange(seg_block.shape[0], dtype=jnp.int32)
    cols_index = jnp.arange(segments_row.shape[0], dtype=jnp.int32)
    return (
        (seg_block[:, None] == segments_row[None, :]) & (cols_index[None, :] <= rows_index[:, None])
    ).astype(jnp.int32)


def masked_softmax(scores, doc_mask):
    masked = jnp.where(doc_mask > 0, scores, -jnp.inf)
    peak = jnp.max(masked, axis=-1, keepdims=True)
    weights = jnp.exp(masked - peak)
    return weights / jnp.sum(weights, axis=-1, keepdims=True)


CHUNKS = 21


def sum_kernel(chunks, g_ref, out_ref, acc, from_core, from_x, result, from_mid, *sems):
    (load_s, core_s, core_r, x_s, x_r, z_s, z_r, mid_s, mid_r) = sems[:9]
    (xg_s, xg_r, own_s, own_r, fwd_s, fwd_r, keep_s) = sems[9:]
    rows = acc.shape[1] // chunks
    me = lax.axis_index("dp")
    core = lax.rem(me, 2)
    x = lax.rem(me // 2, 2)
    z = me // 4
    other_core = me + 1 - 2 * core
    other_x = me + 2 - 4 * x
    pair_z = me + 4 - 8 * lax.rem(z, 2)
    other_mid = (3 - z) * 4 + lax.rem(me, 4)
    is_mid = (z == 1) | (z == 2)
    is_end = (z == 0) | (z == 3)

    def part(k):
        return pl.ds(pl.multiple_of(k * rows, rows), rows)

    def send(src, dst, s, r, k, to):
        return pltpu.make_async_remote_copy(
            src_ref=src,
            dst_ref=dst,
            send_sem=s.at[k],
            recv_sem=r.at[k],
            device_id={"dp": to},
            device_id_type=pl.DeviceIdType.MESH,
        )

    def load(k):
        return pltpu.make_async_copy(g_ref.at[:, core, part(k)], acc.at[:, part(k)], load_s.at[k])

    def core_copy(k):
        return send(
            g_ref.at[:, 1 - core, part(k)], from_core.at[:, part(k)], core_s, core_r, k, other_core
        )

    def x_copy(k):
        return send(acc.at[1 - x, part(k)], from_x.at[part(k)], x_s, x_r, k, other_x)

    def up_copy(k):
        return send(acc.at[x, part(k)], result.at[part(k)], z_s, z_r, k, pair_z)

    def mid_copy(k):
        return send(acc.at[x, part(k)], from_mid.at[part(k)], mid_s, mid_r, k, other_mid)

    def down_copy(k):
        return send(result.at[part(k)], result.at[part(k)], z_s, z_r, k, pair_z)

    def xg_copy(k):
        return send(result.at[part(k)], out_ref.at[x, core, part(k)], xg_s, xg_r, k, other_x)

    def own_copy(k):
        return send(result.at[part(k)], out_ref.at[x, core, part(k)], own_s, own_r, k, other_core)

    def keep(k):
        return pltpu.make_async_copy(
            result.at[part(k)], out_ref.at[x, core, part(k)], keep_s.at[k]
        )

    def fwd_copy(k):
        block = out_ref.at[1 - x, core, part(k)]
        return send(block, block, fwd_s, fwd_r, k, other_core)

    barrier = pltpu.get_barrier_semaphore()
    for device in (other_core, other_x, pair_z):
        pl.semaphore_signal(
            barrier, inc=1, device_id={"dp": device}, device_id_type=pl.DeviceIdType.MESH
        )

    @pl.when(is_mid)
    def _():
        pl.semaphore_signal(
            barrier, inc=1, device_id={"dp": other_mid}, device_id_type=pl.DeviceIdType.MESH
        )
        pl.semaphore_wait(barrier, 4)

    @pl.when(is_end)
    def _():
        pl.semaphore_wait(barrier, 3)

    def stage0(k):
        load(k).start()
        core_copy(k).start()

    def stage1(k):
        load(k).wait()
        core_copy(k).wait_recv()
        acc[:, part(k), :] = acc[:, part(k), :] + from_core[:, part(k), :]
        x_copy(k).start()

    def stage2(k):
        x_copy(k).wait_recv()
        acc[x, part(k), :] = acc[x, part(k), :] + from_x[part(k), :]

        @pl.when(is_end)
        def _():
            up_copy(k).start()

    def stage3(k):
        @pl.when(is_mid)
        def _():
            up_copy(k).wait_recv()
            acc[x, part(k), :] = acc[x, part(k), :] + result[part(k), :]
            mid_copy(k).start()

    def stage4(k):
        @pl.when(is_mid)
        def _():
            mid_copy(k).wait_recv()
            result[part(k), :] = acc[x, part(k), :] + from_mid[part(k), :]
            down_copy(k).start()

    def stage5(k):
        @pl.when(is_end)
        def _():
            down_copy(k).wait_recv()

        xg_copy(k).start()
        own_copy(k).start()
        keep(k).start()

    def stage6(k):
        send(
            result.at[part(k)], out_ref.at[1 - x, core, part(k)], xg_s, xg_r, k, other_x
        ).wait_recv()
        fwd_copy(k).start()

    stages = (stage0, stage1, stage2, stage3, stage4, stage5, stage6)

    @pl.loop(0, chunks + len(stages) - 1)
    def _(t):
        for lag in reversed(range(len(stages))):
            @pl.when((t >= lag) & (t < chunks + lag))
            def _():
                stages[lag](t - lag)

    @pl.loop(0, chunks)
    def _(k):
        core_copy(k).wait_send()
        x_copy(k).wait_send()

        @pl.when(is_end)
        def _():
            up_copy(k).wait_send()

        @pl.when(is_mid)
        def _():
            mid_copy(k).wait_send()
            down_copy(k).wait_send()

        xg_copy(k).wait_send()
        own_copy(k).wait_send()
        keep(k).wait()
        fwd_copy(k).wait_send()
        send(
            result.at[part(k)], out_ref.at[x, 1 - core, part(k)], own_s, own_r, k, other_core
        ).wait_recv()
        send(
            result.at[part(k)], out_ref.at[1 - x, 1 - core, part(k)], fwd_s, fwd_r, k, other_core
        ).wait_recv()


def sum_rows(rows):
    count, width = rows.shape
    quarter = count // 4
    f32 = jnp.float32
    dma = pltpu.SemaphoreType.DMA((CHUNKS,))
    out = pl.pallas_call(
        functools.partial(sum_kernel, CHUNKS),
        out_shape=jax.ShapeDtypeStruct((2, 2, quarter, width), f32),
        in_specs=[pl.BlockSpec(memory_space=pl.ANY)],
        out_specs=pl.BlockSpec(memory_space=pl.ANY),
        scratch_shapes=[
            pltpu.VMEM((2, quarter, width), f32),
            pltpu.VMEM((2, quarter, width), f32),
            pltpu.VMEM((quarter, width), f32),
            pltpu.VMEM((quarter, width), f32),
            pltpu.VMEM((quarter, width), f32),
        ]
        + [dma] * 16,
        compiler_params=pltpu.CompilerParams(
            collective_id=0, has_side_effects=True, vmem_limit_bytes=56 * 2**20
        ),
    )(rows.reshape(2, 2, quarter, width))
    return out.reshape(count, width)


BLOCK = 512


def pack_kernel(down, kup, vup, tokens, latent_grad, rope_grad, latent, nope, value, out):
    f32 = jnp.float32
    over_tokens = (((0,), (0,)), ((), ()))
    step = pl.program_id(0)

    def columns(start):
        return pl.ds(pl.multiple_of((step - start) * BLOCK, BLOCK), BLOCK)

    @pl.when(step < down)
    def _():
        out[...] = lax.dot_general(
            tokens[:, columns(0)], latent_grad[...], over_tokens, preferred_element_type=f32
        )

    @pl.when((step >= down) & (step < down + kup))
    def _():
        out[...] = lax.dot_general(
            latent[...], nope[:, columns(down)], over_tokens, preferred_element_type=f32
        )

    @pl.when((step >= down + kup) & (step < down + kup + vup))
    def _():
        out[...] = lax.dot_general(
            latent[...], value[:, columns(down + kup)], over_tokens, preferred_element_type=f32
        )

    @pl.when(step == down + kup + vup)
    def _():
        rows = rope_grad.shape[0]
        for piece in range(down):
            out[piece * rows : (piece + 1) * rows, :] = jnp.dot(
                rope_grad[...],
                tokens[:, piece * BLOCK : (piece + 1) * BLOCK],
                preferred_element_type=f32,
            )


def unpack_kernel(down, kup, vup, total, grad_down, grad_rope, grad_kup, grad_vup):
    step = pl.program_id(0)

    @pl.when(step < down)
    def _():
        grad_down[...] = total[...]

    @pl.when((step >= down) & (step < down + kup))
    def _():
        grad_kup[...] = total[...]

    @pl.when((step >= down + kup) & (step < down + kup + vup))
    def _():
        grad_vup[...] = total[...]

    @pl.when(step == down + kup + vup)
    def _():
        rows = grad_rope.shape[0]
        for piece in range(down):
            grad_rope[:, piece * BLOCK : (piece + 1) * BLOCK] = total[
                piece * rows : (piece + 1) * rows, :
            ]


def packed_grads(tokens, latent_grad, rope_grad, latent, nope, value):
    f32 = jnp.float32
    down, kup, vup = (a.shape[1] // BLOCK for a in (tokens, nope, value))
    steps = down + kup + vup + 1
    whole = pl.BlockSpec(memory_space=pltpu.VMEM)
    params = pltpu.CompilerParams(vmem_limit_bytes=48 * 2**20)
    packed = pl.pallas_call(
        functools.partial(pack_kernel, down, kup, vup),
        grid=(steps,),
        out_shape=jax.ShapeDtypeStruct((steps * BLOCK, BLOCK), f32),
        in_specs=[whole] * 6,
        out_specs=pl.BlockSpec((BLOCK, BLOCK), lambda i: (i, 0)),
        compiler_params=params,
    )(tokens, latent_grad, rope_grad, latent, nope, value)
    total = sum_rows(packed)
    rope_rows = rope_grad.shape[0]
    return pl.pallas_call(
        functools.partial(unpack_kernel, down, kup, vup),
        grid=(steps,),
        out_shape=(
            jax.ShapeDtypeStruct((down * BLOCK, BLOCK), f32),
            jax.ShapeDtypeStruct((rope_rows, down * BLOCK), f32),
            jax.ShapeDtypeStruct((BLOCK, kup * BLOCK), f32),
            jax.ShapeDtypeStruct((BLOCK, vup * BLOCK), f32),
        ),
        in_specs=[pl.BlockSpec((BLOCK, BLOCK), lambda i: (i, 0))],
        out_specs=(
            pl.BlockSpec((BLOCK, BLOCK), lambda i: (jnp.minimum(i, down - 1), 0)),
            pl.BlockSpec((rope_rows, down * BLOCK), lambda i: (0, 0)),
            pl.BlockSpec((BLOCK, BLOCK), lambda i: (0, jnp.clip(i - down, 0, kup - 1))),
            pl.BlockSpec((BLOCK, BLOCK), lambda i: (0, jnp.clip(i - down - kup, 0, vup - 1))),
        ),
        compiler_params=params,
    )(total)


def local(
    by_kernel,
    tokens,
    segment_ids,
    queries,
    teacher_keys,
    teacher_values,
    down_weight,
    rope_weight,
    key_up,
    value_up,
):
    f32 = jnp.float32
    bf16 = jnp.bfloat16
    token_rows = tokens[0]
    segments_row = segment_ids[0]
    seq_len = token_rows.shape[0]
    heads_local = queries.shape[2] // HEAD
    kv_local = teacher_keys.shape[2] // HEAD
    group_size = heads_local // kv_local
    nope_width = HEAD - ROPE
    score_scale = 1.0 / math.sqrt(HEAD)
    contract_cols = (((1,), (1,)), ((), ()))
    contract_rows = (((0,), (0,)), ((), ()))
    positions = doc_positions(segments_row)
    cos_full, sin_full = angle_tables(positions, HEAD)
    cos_rope, sin_rope = angle_tables(positions, ROPE)
    latent_part = jnp.dot(token_rows, down_weight, preferred_element_type=f32)
    rope_part = lax.dot_general(rope_weight, token_rows, contract_cols, preferred_element_type=f32)
    latent_raw, rope_sum = lax.psum((latent_part, rope_part), "tensor")
    inv_rms = lax.rsqrt(jnp.mean(latent_raw * latent_raw, axis=-1, keepdims=True) + norm_eps)
    normed = latent_raw * inv_rms
    latent = normed.astype(bf16)
    rope_key = rotate_rows(rope_sum, cos_rope.T, sin_rope.T).astype(bf16)
    head_queries = queries[0].reshape(seq_len, heads_local, HEAD).transpose(1, 0, 2)
    teacher_q = (
        rotate_last(head_queries.astype(f32), cos_full, sin_full)
        .astype(bf16)
        .reshape(kv_local, group_size, seq_len, HEAD)
    )
    teacher_k = rotate_last(
        teacher_keys[0].reshape(seq_len, kv_local, HEAD).transpose(1, 0, 2).astype(f32),
        cos_full,
        sin_full,
    ).astype(bf16)
    teacher_v = teacher_values[0].reshape(seq_len, kv_local, HEAD).transpose(1, 0, 2)
    key_nope = (
        jnp.dot(latent, key_up, preferred_element_type=f32)
        .astype(bf16)
        .reshape(seq_len, heads_local, nope_width)
        .transpose(1, 0, 2)
    )
    head_values = (
        jnp.dot(latent, value_up, preferred_element_type=f32)
        .astype(bf16)
        .reshape(seq_len, heads_local, HEAD)
        .transpose(1, 0, 2)
    )
    rotated_q = rotate_last(head_queries[..., :ROPE].astype(f32), cos_rope, sin_rope).astype(bf16)
    student_q = jnp.concatenate([head_queries[..., ROPE:], rotated_q], axis=-1)
    student_k = jnp.concatenate(
        [key_nope, jnp.broadcast_to(rope_key.T[None], (heads_local, seq_len, ROPE))], axis=-1
    )
    block_rows = min(seq_len, 512)
    block_count = seq_len // block_rows

    def attend_block(carry, block_index):
        value_acc, key_acc = carry
        row_start = block_index * block_rows
        doc_mask = block_mask(segments_row, segments_row, row_start)
        teacher_scores = (
            jnp.einsum("kgqd,kpd->kgqp", teacher_q, teacher_k, preferred_element_type=f32)
            * score_scale
        )
        teacher_weights = masked_softmax(teacher_scores, doc_mask).astype(bf16)
        teacher_out = jnp.einsum(
            "kgqp,kpd->kgqd", teacher_weights, teacher_v, preferred_element_type=f32
        ).reshape(heads_local, block_rows, HEAD)
        student_scores = (
            jnp.einsum("hqd,hpd->hqp", student_q, student_k, preferred_element_type=f32)
            * score_scale
        )
        student_weights = masked_softmax(student_scores, doc_mask)
        student_low = student_weights.astype(bf16)
        student_out = jnp.einsum(
            "hqp,hpd->hqd", student_low, head_values, preferred_element_type=f32
        )
        out_grad = (student_out - teacher_out).astype(bf16)
        weight_grad = jnp.einsum("hqd,hpd->hqp", out_grad, head_values, preferred_element_type=f32)
        row_dot = jnp.sum(student_weights * weight_grad, axis=-1, keepdims=True)
        score_grad = (student_weights * (weight_grad - row_dot) * score_scale).astype(bf16)
        value_acc = value_acc + jnp.einsum(
            "hqp,hqd->hpd", student_low, out_grad, preferred_element_type=f32
        )
        key_acc = key_acc + jnp.einsum(
            "hqp,hqd->hpd", score_grad, student_q, preferred_element_type=f32
        )
        return ((value_acc, key_acc), None)

    zeros_acc = jnp.zeros((heads_local, seq_len, HEAD), f32)
    accums, unused = lax.scan(
        attend_block, (zeros_acc, zeros_acc), jnp.arange(block_count, dtype=jnp.int32)
    )
    value_acc, key_acc = accums
    value_flat = value_acc.astype(bf16).transpose(1, 0, 2).reshape(seq_len, heads_local * HEAD)
    nope_grad = (
        key_acc[..., :nope_width]
        .astype(bf16)
        .transpose(1, 0, 2)
        .reshape(seq_len, heads_local * nope_width)
    )
    rope_grad_part = jnp.sum(key_acc[..., nope_width:], axis=0).T
    norm_grad_part = lax.dot_general(
        nope_grad, key_up, contract_cols, preferred_element_type=f32
    ) + lax.dot_general(value_flat, value_up, contract_cols, preferred_element_type=f32)
    norm_grad, rope_grad_sum = lax.psum((norm_grad_part, rope_grad_part), "tensor")
    latent_grad = (
        (norm_grad - normed * jnp.mean(norm_grad * normed, axis=-1, keepdims=True)) * inv_rms
    ).astype(bf16)
    rope_grad = unrotate_rows(rope_grad_sum, cos_rope.T, sin_rope.T).astype(bf16)
    if by_kernel:
        return packed_grads(token_rows, latent_grad, rope_grad, latent, nope_grad, value_flat)
    grad_kup = lax.dot_general(latent, nope_grad, contract_rows, preferred_element_type=f32)
    grad_vup = lax.dot_general(latent, value_flat, contract_rows, preferred_element_type=f32)
    grad_down = lax.dot_general(token_rows, latent_grad, contract_rows, preferred_element_type=f32)
    grad_rope = jnp.dot(rope_grad, token_rows, preferred_element_type=f32)
    return lax.psum((grad_down, grad_rope, grad_kup, grad_vup), "dp")


def solution(mesh):
    in_specs = (
        P("dp", None, "tensor"),
        P("dp", None),
        P("dp", None, "tensor"),
        P("dp", None, "tensor"),
        P("dp", None, "tensor"),
        P("tensor", None),
        P(None, "tensor"),
        P(None, "tensor"),
        P(None, "tensor"),
    )
    out_specs = (P("tensor", None), P(None, "tensor"), P(None, "tensor"), P(None, "tensor"))
    by_kernel = mesh.shape["dp"] == 16 and mesh.shape["tensor"] == 2
    body = functools.partial(local, by_kernel)
    return jax.shard_map(body, mesh=mesh, in_specs=in_specs, out_specs=out_specs, check_vma=False)
```

```python
import functools
import math

import jax
import jax.numpy as jnp
from jax import lax
from jax.experimental import pallas as pl
from jax.experimental.pallas import tpu as pltpu
from jax.sharding import PartitionSpec as P

HEAD = 128
ROPE = 64


theta_base = 500000.0
norm_eps = 1e-06


def angle_tables(positions, width):
    half_width = width // 2
    exponent = jnp.arange(half_width, dtype=jnp.float32) * (2.0 / width)
    frequency = jnp.exp(-exponent * jnp.log(jnp.float32(theta_base)))
    angles = positions.astype(jnp.float32)[:, None] * frequency[None, :]
    return (jnp.cos(angles), jnp.sin(angles))


def rotate_last(tensor, cosine, sine_tab):
    half_width = tensor.shape[-1] // 2
    first_half = tensor[..., :half_width]
    second_half = tensor[..., half_width:]
    return jnp.concatenate(
        [
            first_half * cosine - second_half * sine_tab,
            second_half * cosine + first_half * sine_tab,
        ],
        axis=-1,
    )


def rotate_rows(matrix, cosine, sine_tab):
    half_width = matrix.shape[0] // 2
    first_half = matrix[:half_width]
    second_half = matrix[half_width:]
    return jnp.concatenate(
        [
            first_half * cosine - second_half * sine_tab,
            second_half * cosine + first_half * sine_tab,
        ],
        axis=0,
    )


def unrotate_rows(matrix, cosine, sine_tab):
    half_width = matrix.shape[0] // 2
    first_half = matrix[:half_width]
    second_half = matrix[half_width:]
    return jnp.concatenate(
        [
            first_half * cosine + second_half * sine_tab,
            second_half * cosine - first_half * sine_tab,
        ],
        axis=0,
    )


def doc_positions(segments_row):
    position_index = jnp.arange(segments_row.shape[0], dtype=jnp.int32)
    earlier = (segments_row[None, :] < segments_row[:, None]).astype(jnp.int32)
    return position_index - jnp.sum(earlier, axis=1)


def block_mask(seg_block, segments_row, row_start):
    rows_index = row_start + jnp.arange(seg_block.shape[0], dtype=jnp.int32)
    cols_index = jnp.arange(segments_row.shape[0], dtype=jnp.int32)
    return (
        (seg_block[:, None] == segments_row[None, :]) & (cols_index[None, :] <= rows_index[:, None])
    ).astype(jnp.int32)


def masked_softmax(scores, doc_mask):
    masked = jnp.where(doc_mask > 0, scores, -jnp.inf)
    peak = jnp.max(masked, axis=-1, keepdims=True)
    weights = jnp.exp(masked - peak)
    return weights / jnp.sum(weights, axis=-1, keepdims=True)


CHUNKS = 21


def sum_kernel(chunks, g_ref, out_ref, acc, from_core, from_x, result, from_mid, *sems):
    (load_s, core_s, core_r, x_s, x_r, z_s, z_r, mid_s, mid_r) = sems[:9]
    (xg_s, xg_r, own_s, own_r, fwd_s, fwd_r, keep_s) = sems[9:]
    rows = acc.shape[1] // chunks
    me = lax.axis_index("dp")
    core = lax.rem(me, 2)
    x = lax.rem(me // 2, 2)
    z = me // 4
    other_core = me + 1 - 2 * core
    other_x = me + 2 - 4 * x
    pair_z = me + 4 - 8 * lax.rem(z, 2)
    other_mid = (3 - z) * 4 + lax.rem(me, 4)
    is_mid = (z == 1) | (z == 2)
    is_end = (z == 0) | (z == 3)

    def part(k):
        return pl.ds(pl.multiple_of(k * rows, rows), rows)

    def send(src, dst, s, r, k, to):
        return pltpu.make_async_remote_copy(
            src_ref=src,
            dst_ref=dst,
            send_sem=s.at[k],
            recv_sem=r.at[k],
            device_id={"dp": to},
            device_id_type=pl.DeviceIdType.MESH,
        )

    def load(k):
        return pltpu.make_async_copy(g_ref.at[:, core, part(k)], acc.at[:, part(k)], load_s.at[k])

    def core_copy(k):
        return send(
            g_ref.at[:, 1 - core, part(k)], from_core.at[:, part(k)], core_s, core_r, k, other_core
        )

    def x_copy(k):
        return send(acc.at[1 - x, part(k)], from_x.at[part(k)], x_s, x_r, k, other_x)

    def up_copy(k):
        return send(acc.at[x, part(k)], result.at[part(k)], z_s, z_r, k, pair_z)

    def mid_copy(k):
        return send(acc.at[x, part(k)], from_mid.at[part(k)], mid_s, mid_r, k, other_mid)

    def down_copy(k):
        return send(result.at[part(k)], result.at[part(k)], z_s, z_r, k, pair_z)

    def xg_copy(k):
        return send(result.at[part(k)], out_ref.at[x, core, part(k)], xg_s, xg_r, k, other_x)

    def own_copy(k):
        return send(result.at[part(k)], out_ref.at[x, core, part(k)], own_s, own_r, k, other_core)

    def keep(k):
        return pltpu.make_async_copy(
            result.at[part(k)], out_ref.at[x, core, part(k)], keep_s.at[k]
        )

    def fwd_copy(k):
        block = out_ref.at[1 - x, core, part(k)]
        return send(block, block, fwd_s, fwd_r, k, other_core)

    barrier = pltpu.get_barrier_semaphore()
    for device in (other_core, other_x, pair_z):
        pl.semaphore_signal(
            barrier, inc=1, device_id={"dp": device}, device_id_type=pl.DeviceIdType.MESH
        )

    @pl.when(is_mid)
    def _():
        pl.semaphore_signal(
            barrier, inc=1, device_id={"dp": other_mid}, device_id_type=pl.DeviceIdType.MESH
        )
        pl.semaphore_wait(barrier, 4)

    @pl.when(is_end)
    def _():
        pl.semaphore_wait(barrier, 3)

    def stage0(k):
        load(k).start()
        core_copy(k).start()

    def stage1(k):
        load(k).wait()
        core_copy(k).wait_recv()
        acc[:, part(k), :] = acc[:, part(k), :] + from_core[:, part(k), :]
        x_copy(k).start()

    def stage2(k):
        x_copy(k).wait_recv()
        acc[x, part(k), :] = acc[x, part(k), :] + from_x[part(k), :]

        @pl.when(is_end)
        def _():
            up_copy(k).start()

    def stage3(k):
        @pl.when(is_mid)
        def _():
            up_copy(k).wait_recv()
            acc[x, part(k), :] = acc[x, part(k), :] + result[part(k), :]
            mid_copy(k).start()

    def stage4(k):
        @pl.when(is_mid)
        def _():
            mid_copy(k).wait_recv()
            result[part(k), :] = acc[x, part(k), :] + from_mid[part(k), :]
            down_copy(k).start()

    def stage5(k):
        @pl.when(is_end)
        def _():
            down_copy(k).wait_recv()

        xg_copy(k).start()
        own_copy(k).start()
        keep(k).start()

    def stage6(k):
        send(
            result.at[part(k)], out_ref.at[1 - x, core, part(k)], xg_s, xg_r, k, other_x
        ).wait_recv()
        fwd_copy(k).start()

    stages = (stage0, stage1, stage2, stage3, stage4, stage5, stage6)

    @pl.loop(0, chunks + len(stages) - 1)
    def _(t):
        for lag in reversed(range(len(stages))):
            @pl.when((t >= lag) & (t < chunks + lag))
            def _():
                stages[lag](t - lag)

    @pl.loop(0, chunks)
    def _(k):
        core_copy(k).wait_send()
        x_copy(k).wait_send()

        @pl.when(is_end)
        def _():
            up_copy(k).wait_send()

        @pl.when(is_mid)
        def _():
            mid_copy(k).wait_send()
            down_copy(k).wait_send()

        xg_copy(k).wait_send()
        own_copy(k).wait_send()
        keep(k).wait()
        fwd_copy(k).wait_send()
        send(
            result.at[part(k)], out_ref.at[x, 1 - core, part(k)], own_s, own_r, k, other_core
        ).wait_recv()
        send(
            result.at[part(k)], out_ref.at[1 - x, 1 - core, part(k)], fwd_s, fwd_r, k, other_core
        ).wait_recv()


def sum_rows(rows):
    count, width = rows.shape
    quarter = count // 4
    f32 = jnp.float32
    dma = pltpu.SemaphoreType.DMA((CHUNKS,))
    out = pl.pallas_call(
        functools.partial(sum_kernel, CHUNKS),
        out_shape=jax.ShapeDtypeStruct((2, 2, quarter, width), f32),
        in_specs=[pl.BlockSpec(memory_space=pl.ANY)],
        out_specs=pl.BlockSpec(memory_space=pl.ANY),
        scratch_shapes=[
            pltpu.VMEM((2, quarter, width), f32),
            pltpu.VMEM((2, quarter, width), f32),
            pltpu.VMEM((quarter, width), f32),
            pltpu.VMEM((quarter, width), f32),
            pltpu.VMEM((quarter, width), f32),
        ]
        + [dma] * 16,
        compiler_params=pltpu.CompilerParams(
            collective_id=0, has_side_effects=True, vmem_limit_bytes=56 * 2**20
        ),
    )(rows.reshape(2, 2, quarter, width))
    return out.reshape(count, width)


BLOCK = 512


def pack_kernel(down, kup, vup, tokens, latent_grad, rope_grad, latent, nope, value, out):
    f32 = jnp.float32
    over_tokens = (((0,), (0,)), ((), ()))
    step = pl.program_id(0)

    def columns(start):
        return pl.ds(pl.multiple_of((step - start) * BLOCK, BLOCK), BLOCK)

    @pl.when(step < down)
    def _():
        out[...] = lax.dot_general(
            tokens[:, columns(0)], latent_grad[...], over_tokens, preferred_element_type=f32
        )

    @pl.when((step >= down) & (step < down + kup))
    def _():
        out[...] = lax.dot_general(
            latent[...], nope[:, columns(down)], over_tokens, preferred_element_type=f32
        )

    @pl.when((step >= down + kup) & (step < down + kup + vup))
    def _():
        out[...] = lax.dot_general(
            latent[...], value[:, columns(down + kup)], over_tokens, preferred_element_type=f32
        )

    @pl.when(step == down + kup + vup)
    def _():
        rows = rope_grad.shape[0]
        for piece in range(down):
            out[piece * rows : (piece + 1) * rows, :] = jnp.dot(
                rope_grad[...],
                tokens[:, piece * BLOCK : (piece + 1) * BLOCK],
                preferred_element_type=f32,
            )


def unpack_kernel(down, kup, vup, total, grad_down, grad_rope, grad_kup, grad_vup):
    step = pl.program_id(0)

    @pl.when(step < down)
    def _():
        grad_down[...] = total[...]

    @pl.when((step >= down) & (step < down + kup))
    def _():
        grad_kup[...] = total[...]

    @pl.when((step >= down + kup) & (step < down + kup + vup))
    def _():
        grad_vup[...] = total[...]

    @pl.when(step == down + kup + vup)
    def _():
        rows = grad_rope.shape[0]
        for piece in range(down):
            grad_rope[:, piece * BLOCK : (piece + 1) * BLOCK] = total[
                piece * rows : (piece + 1) * rows, :
            ]


def packed_grads(tokens, latent_grad, rope_grad, latent, nope, value):
    f32 = jnp.float32
    down, kup, vup = (a.shape[1] // BLOCK for a in (tokens, nope, value))
    steps = down + kup + vup + 1
    whole = pl.BlockSpec(memory_space=pltpu.VMEM)
    params = pltpu.CompilerParams(vmem_limit_bytes=48 * 2**20)
    packed = pl.pallas_call(
        functools.partial(pack_kernel, down, kup, vup),
        grid=(steps,),
        out_shape=jax.ShapeDtypeStruct((steps * BLOCK, BLOCK), f32),
        in_specs=[whole] * 6,
        out_specs=pl.BlockSpec((BLOCK, BLOCK), lambda i: (i, 0)),
        compiler_params=params,
    )(tokens, latent_grad, rope_grad, latent, nope, value)
    total = sum_rows(packed)
    rope_rows = rope_grad.shape[0]
    return pl.pallas_call(
        functools.partial(unpack_kernel, down, kup, vup),
        grid=(steps,),
        out_shape=(
            jax.ShapeDtypeStruct((down * BLOCK, BLOCK), f32),
            jax.ShapeDtypeStruct((rope_rows, down * BLOCK), f32),
            jax.ShapeDtypeStruct((BLOCK, kup * BLOCK), f32),
            jax.ShapeDtypeStruct((BLOCK, vup * BLOCK), f32),
        ),
        in_specs=[pl.BlockSpec((BLOCK, BLOCK), lambda i: (i, 0))],
        out_specs=(
            pl.BlockSpec((BLOCK, BLOCK), lambda i: (jnp.minimum(i, down - 1), 0)),
            pl.BlockSpec((rope_rows, down * BLOCK), lambda i: (0, 0)),
            pl.BlockSpec((BLOCK, BLOCK), lambda i: (0, jnp.clip(i - down, 0, kup - 1))),
            pl.BlockSpec((BLOCK, BLOCK), lambda i: (0, jnp.clip(i - down - kup, 0, vup - 1))),
        ),
        compiler_params=params,
    )(total)


def tensor_sum(parts, is_pair):
    if not is_pair:
        return lax.psum(parts, "tensor")
    return tuple(part + lax.ppermute(part, "tensor", ((0, 1), (1, 0))) for part in parts)


def local(
    by_kernel,
    tokens,
    segment_ids,
    queries,
    teacher_keys,
    teacher_values,
    down_weight,
    rope_weight,
    key_up,
    value_up,
):
    f32 = jnp.float32
    bf16 = jnp.bfloat16
    token_rows = tokens[0]
    segments_row = segment_ids[0]
    seq_len = token_rows.shape[0]
    heads_local = queries.shape[2] // HEAD
    kv_local = teacher_keys.shape[2] // HEAD
    group_size = heads_local // kv_local
    nope_width = HEAD - ROPE
    score_scale = 1.0 / math.sqrt(HEAD)
    contract_cols = (((1,), (1,)), ((), ()))
    contract_rows = (((0,), (0,)), ((), ()))
    positions = doc_positions(segments_row)
    cos_full, sin_full = angle_tables(positions, HEAD)
    cos_rope, sin_rope = angle_tables(positions, ROPE)
    latent_part = jnp.dot(token_rows, down_weight, preferred_element_type=f32)
    rope_part = lax.dot_general(rope_weight, token_rows, contract_cols, preferred_element_type=f32)
    latent_raw, rope_sum = tensor_sum((latent_part, rope_part), by_kernel)
    inv_rms = lax.rsqrt(jnp.mean(latent_raw * latent_raw, axis=-1, keepdims=True) + norm_eps)
    normed = latent_raw * inv_rms
    latent = normed.astype(bf16)
    rope_key = rotate_rows(rope_sum, cos_rope.T, sin_rope.T).astype(bf16)
    head_queries = queries[0].reshape(seq_len, heads_local, HEAD).transpose(1, 0, 2)
    teacher_q = (
        rotate_last(head_queries.astype(f32), cos_full, sin_full)
        .astype(bf16)
        .reshape(kv_local, group_size, seq_len, HEAD)
    )
    teacher_k = rotate_last(
        teacher_keys[0].reshape(seq_len, kv_local, HEAD).transpose(1, 0, 2).astype(f32),
        cos_full,
        sin_full,
    ).astype(bf16)
    teacher_v = teacher_values[0].reshape(seq_len, kv_local, HEAD).transpose(1, 0, 2)
    key_nope = (
        jnp.dot(latent, key_up, preferred_element_type=f32)
        .astype(bf16)
        .reshape(seq_len, heads_local, nope_width)
        .transpose(1, 0, 2)
    )
    head_values = (
        jnp.dot(latent, value_up, preferred_element_type=f32)
        .astype(bf16)
        .reshape(seq_len, heads_local, HEAD)
        .transpose(1, 0, 2)
    )
    rotated_q = rotate_last(head_queries[..., :ROPE].astype(f32), cos_rope, sin_rope).astype(bf16)
    student_q = jnp.concatenate([head_queries[..., ROPE:], rotated_q], axis=-1)
    student_k = jnp.concatenate(
        [key_nope, jnp.broadcast_to(rope_key.T[None], (heads_local, seq_len, ROPE))], axis=-1
    )
    block_rows = min(seq_len, 512)
    block_count = seq_len // block_rows

    def attend_block(carry, block_index):
        value_acc, key_acc = carry
        row_start = block_index * block_rows
        doc_mask = block_mask(segments_row, segments_row, row_start)
        teacher_scores = (
            jnp.einsum("kgqd,kpd->kgqp", teacher_q, teacher_k, preferred_element_type=f32)
            * score_scale
        )
        teacher_weights = masked_softmax(teacher_scores, doc_mask).astype(bf16)
        teacher_out = jnp.einsum(
            "kgqp,kpd->kgqd", teacher_weights, teacher_v, preferred_element_type=f32
        ).reshape(heads_local, block_rows, HEAD)
        student_scores = (
            jnp.einsum("hqd,hpd->hqp", student_q, student_k, preferred_element_type=f32)
            * score_scale
        )
        student_weights = masked_softmax(student_scores, doc_mask)
        student_low = student_weights.astype(bf16)
        student_out = jnp.einsum(
            "hqp,hpd->hqd", student_low, head_values, preferred_element_type=f32
        )
        out_grad = (student_out - teacher_out).astype(bf16)
        weight_grad = jnp.einsum("hqd,hpd->hqp", out_grad, head_values, preferred_element_type=f32)
        row_dot = jnp.sum(student_weights * weight_grad, axis=-1, keepdims=True)
        score_grad = (student_weights * (weight_grad - row_dot) * score_scale).astype(bf16)
        value_acc = value_acc + jnp.einsum(
            "hqp,hqd->hpd", student_low, out_grad, preferred_element_type=f32
        )
        key_acc = key_acc + jnp.einsum(
            "hqp,hqd->hpd", score_grad, student_q, preferred_element_type=f32
        )
        return ((value_acc, key_acc), None)

    zeros_acc = jnp.zeros((heads_local, seq_len, HEAD), f32)
    accums, unused = lax.scan(
        attend_block, (zeros_acc, zeros_acc), jnp.arange(block_count, dtype=jnp.int32)
    )
    value_acc, key_acc = accums
    value_flat = value_acc.astype(bf16).transpose(1, 0, 2).reshape(seq_len, heads_local * HEAD)
    nope_grad = (
        key_acc[..., :nope_width]
        .astype(bf16)
        .transpose(1, 0, 2)
        .reshape(seq_len, heads_local * nope_width)
    )
    rope_grad_part = jnp.sum(key_acc[..., nope_width:], axis=0).T
    norm_grad_part = lax.dot_general(
        nope_grad, key_up, contract_cols, preferred_element_type=f32
    ) + lax.dot_general(value_flat, value_up, contract_cols, preferred_element_type=f32)
    norm_grad, rope_grad_sum = tensor_sum((norm_grad_part, rope_grad_part), by_kernel)
    latent_grad = (
        (norm_grad - normed * jnp.mean(norm_grad * normed, axis=-1, keepdims=True)) * inv_rms
    ).astype(bf16)
    rope_grad = unrotate_rows(rope_grad_sum, cos_rope.T, sin_rope.T).astype(bf16)
    if by_kernel:
        return packed_grads(token_rows, latent_grad, rope_grad, latent, nope_grad, value_flat)
    grad_kup = lax.dot_general(latent, nope_grad, contract_rows, preferred_element_type=f32)
    grad_vup = lax.dot_general(latent, value_flat, contract_rows, preferred_element_type=f32)
    grad_down = lax.dot_general(token_rows, latent_grad, contract_rows, preferred_element_type=f32)
    grad_rope = jnp.dot(rope_grad, token_rows, preferred_element_type=f32)
    return lax.psum((grad_down, grad_rope, grad_kup, grad_vup), "dp")


def solution(mesh):
    in_specs = (
        P("dp", None, "tensor"),
        P("dp", None),
        P("dp", None, "tensor"),
        P("dp", None, "tensor"),
        P("dp", None, "tensor"),
        P("tensor", None),
        P(None, "tensor"),
        P(None, "tensor"),
        P(None, "tensor"),
    )
    out_specs = (P("tensor", None), P(None, "tensor"), P(None, "tensor"), P(None, "tensor"))
    by_kernel = mesh.shape["dp"] == 16 and mesh.shape["tensor"] == 2
    body = functools.partial(local, by_kernel)
    return jax.shard_map(body, mesh=mesh, in_specs=in_specs, out_specs=out_specs, check_vma=False)
```
